32 devices in a mesh: chan: 16 (over z, x, core), hour: 2 (over y).
Axes of the slice: x: 2, y: 2, z: 4, core: 2. Of those that a mesh axis runs over, the one named last changes fastest.
Arguments:
- samples: bfloat16 [2, 24, 2048, 256], P('hour', None, 'chan'), may hold values from -180 to 180
- masks: int32 [2], replicated, may hold values from 1 to 15, as said below
Outputs:
- stacked: float32 [2, 128, 2048, 256], P(None, 'hour', 'chan')
The draws below stay inside these ranges and needn't reach their ends.
Inputs may be any that keep to these rules, and one draw needn't show every extreme that they name: `masks`: the 2 values differ, and one of them is 15.
All inputs are finite; a program needn't handle non-finite values.
Results may differ from the reference program's by a relative error of at most 0.015.
Values may be sent and summed in bfloat16 or wider, within the bound.
A program may use at most 192 MiB of HBM per device.

```python
import math
import jax
import jax.numpy as jnp
from jax import lax

F = 128
LENGTH = 256
W = 24
CB = 128
ROUNDS = 2
HOURS = 2
CHANNELS = 2048
N_CHAN = 16


def draw_samples(key, part):
    key = jax.random.fold_in(key, 11)
    first, second = jax.random.split(key, 2)
    shape = (HOURS, W, CHANNELS, LENGTH)
    base = jnp.clip(jax.random.normal(first, shape, jnp.float32), -6.0, 6.0)
    spread = jax.random.uniform(second, (HOURS, W, CHANNELS, 1), jnp.float32) * math.log(10.0)
    return (base * jnp.exp(spread)).astype(jnp.bfloat16)


def draw_masks(key, part):
    key = jax.random.fold_in(key, 23)
    first, second = jax.random.split(key, 2)
    others = jax.random.randint(first, (ROUNDS,), 1, N_CHAN - 1)
    position = jax.random.randint(second, (), 0, ROUNDS)
    places = jnp.arange(ROUNDS, dtype=jnp.int32)
    return jnp.where(places == position, N_CHAN - 1, others).astype(jnp.int32)


def setup_inputs(seed: int = 0) -> dict:
    splits = jax.random.split(jax.random.key(seed), 3)
    return {
        "samples": draw_samples(jax.random.fold_in(splits[2], 71), 0),
        "masks": draw_masks(jax.random.fold_in(splits[2], 71), 0),
    }


def dft_table(length, bin_count):
    sample_index = lax.broadcasted_iota(jnp.int32, (length, bin_count), 0)
    bin_index = lax.broadcasted_iota(jnp.int32, (length, bin_count), 1)
    phase_angle = (sample_index * bin_index % length).astype(jnp.float32) * (2.0 * math.pi / length)
    return jnp.concatenate([jnp.cos(phase_angle), -jnp.sin(phase_angle)], axis=1).astype(jnp.bfloat16)

def whiten_all(series):
    dft_rows = dft_table(LENGTH, F).astype(jnp.float32)
    spectrum = jnp.einsum('wcl,lk->kwc', series.astype(jnp.float32), dft_rows)
    real_part = spectrum[:F]
    imag_part = spectrum[F:]
    power_mean = lax.optimization_barrier(jnp.mean(real_part * real_part + imag_part * imag_part, axis=0))
    inverse_rms = lax.rsqrt(power_mean + 1e-06)
    real_part = (real_part * inverse_rms).reshape(F, W, N_CHAN, CB)
    imag_part = (imag_part * inverse_rms).reshape(F, W, N_CHAN, CB)
    return jnp.concatenate([real_part, imag_part], axis=3).astype(jnp.bfloat16)

def cross_spectra(own_block, partner_block):
    products = jnp.einsum('fwa,fwb->fab', own_block.astype(jnp.float32), partner_block.astype(jnp.float32))
    half_width = own_block.shape[2] // 2
    real_cross = products[:, :half_width, :half_width] + products[:, half_width:, half_width:]
    imag_cross = products[:, half_width:, :half_width] - products[:, :half_width, half_width:]
    return jnp.concatenate([real_cross, imag_cross], axis=2)

def reference(samples, masks):
    factor = 1.0 / math.sqrt(W * HOURS)
    block_ids = jnp.arange(N_CHAN, dtype=jnp.int32)
    totals = jnp.zeros((ROUNDS, F, N_CHAN, CB, 2 * CB), jnp.float32)
    for hour_index in range(HOURS):
        spectrum = whiten_all(samples[hour_index])
        blocks = jnp.moveaxis(spectrum, 2, 0)
        for round_index in range(ROUNDS):
            partner_ids = jnp.bitwise_xor(block_ids, masks[round_index]).astype(jnp.int32)
            partners = jnp.take(blocks, partner_ids, axis=0)
            result = lax.map(lambda both: cross_spectra(both[0], both[1]), (blocks, partners))
            rounded = (result * factor).astype(jnp.bfloat16)
            rounded = lax.optimization_barrier(rounded)
            totals = totals.at[round_index].add(jnp.moveaxis(rounded.astype(jnp.float32), 0, 1))
    return totals.reshape(ROUNDS, F, N_CHAN * CB, 2 * CB)
```

```python
import functools
import math

import jax
import jax.numpy as jnp
from jax import lax
from jax.experimental import pallas as pl
from jax.experimental.pallas import tpu as pltpu
from jax.sharding import PartitionSpec as P

SPLITS = 4


def dft_table(length, bin_count):
    sample_index = lax.broadcasted_iota(jnp.int32, (length, bin_count), 0)
    bin_index = lax.broadcasted_iota(jnp.int32, (length, bin_count), 1)
    phase_angle = (sample_index * bin_index % length).astype(jnp.float32) * (2.0 * math.pi / length)
    return jnp.concatenate([jnp.cos(phase_angle), -jnp.sin(phase_angle)], axis=1).astype(
        jnp.bfloat16
    )


def whiten(series, bin_count):
    dft_rows = dft_table(series.shape[2], bin_count)
    spectrum = jnp.einsum("wcl,lk->kwc", series, dft_rows, preferred_element_type=jnp.float32)
    real_part = spectrum[:bin_count]
    imag_part = spectrum[bin_count:]
    power_mean = jnp.mean(real_part * real_part + imag_part * imag_part, axis=0)
    inverse_rms = lax.rsqrt(power_mean + 1e-06)
    return jnp.concatenate([real_part * inverse_rms, imag_part * inverse_rms], axis=2).astype(
        jnp.bfloat16
    )


def cross_kernel(hours, factor, place_ref, *refs):
    own_refs, partner_refs = refs[:hours], refs[hours : 2 * hours]
    out_ref = refs[-1]
    half = out_ref.shape[2]

    def one_bin(f, carry):
        own = [ref[f].astype(jnp.float32) for ref in own_refs]
        partner = [ref[f].astype(jnp.float32) for ref in partner_refs]
        left = jnp.concatenate([o[:, :half] for o in own] + [o[:, half:] for o in own], axis=0)
        real_q = jnp.concatenate([q[:, :half] for q in partner] + [q[:, half:] for q in partner], axis=0)
        imag_q = jnp.concatenate([-q[:, half:] for q in partner] + [q[:, :half] for q in partner], axis=0)
        right = jnp.concatenate([real_q, imag_q], axis=1)
        product = lax.dot_general(
            left.astype(jnp.bfloat16),
            right.astype(jnp.bfloat16),
            (((0,), (0,)), ((), ())),
            preferred_element_type=jnp.float32,
        )
        out_ref[0, f] = product * factor
        return carry

    lax.fori_loop(0, out_ref.shape[1], one_bin, 0, unroll=True)


def cross_into(total, shape, place, start, own, partner, partner_starts, factor):
    bins = min(p.shape[0] for p in partner)
    tile = min(8, bins)
    groups = len(own)

    def spec(array, offset):
        return pl.BlockSpec((tile,) + array.shape[1:], lambda i, p: (i + offset // tile, 0, 0))

    out_spec = pl.BlockSpec((1, tile) + shape[2:], lambda i, p: (p[0], i + start // tile, 0, 0))
    operands = [place, *own, *partner]
    in_specs = [spec(o, start) for o in own] + [spec(q, o) for q, o in zip(partner, partner_starts)]
    aliases = {}
    if total is not None:
        aliases = {len(operands): 0}
        operands.append(total)
        in_specs.append(pl.BlockSpec(memory_space=pl.ANY))
    rows = sum(o.shape[1] for o in own)
    return pl.pallas_call(
        functools.partial(cross_kernel, groups, factor),
        out_shape=jax.ShapeDtypeStruct(shape, jnp.float32),
        grid_spec=pltpu.PrefetchScalarGridSpec(
            num_scalar_prefetch=1,
            grid=(bins // tile,),
            in_specs=in_specs,
            out_specs=out_spec,
        ),
        input_output_aliases=aliases,
        compiler_params=pltpu.CompilerParams(vmem_limit_bytes=32 * 1024 * 1024),
        cost_estimate=pl.CostEstimate(
            flops=2 * bins * rows * shape[3] * shape[3],
            bytes_accessed=bins * shape[2] * shape[3] * 4,
            transcendentals=0,
        ),
        name="cross",
    )(*operands)


def move(value, mask):
    blocks = lax.axis_size("chan")
    return lax.ppermute(value, "chan", [(i, i ^ mask) for i in range(blocks)])


def on_device(samples, masks):
    bin_count = samples.shape[3] // 2
    hours = lax.axis_size("hour")
    blocks = lax.axis_size("chan")
    owned = bin_count // hours
    factor = 1.0 / math.sqrt(samples.shape[1] * hours)
    far, top = blocks - 1, blocks // 2
    far_first = masks[0] == far
    other = jnp.where(far_first, masks[1], masks[0])
    crosses = other >= top
    near = jnp.where(crosses, other ^ far, other)
    far_place = jnp.where(far_first, 0, 1).astype(jnp.int32).reshape(1)
    near_place = 1 - far_place

    spectra = whiten(samples[0], bin_count)
    hour = lax.axis_index("hour")
    pieces = []
    for apart in range(hours):
        piece = lax.dynamic_slice_in_dim(spectra, (hour + apart) % hours * owned, owned, 0)
        if apart:
            piece = lax.ppermute(piece, "hour", [(i, (i + apart) % hours) for i in range(hours)])
        pieces.append(piece)
    own = [pieces[0], pieces[1] if hours == 2 else jnp.concatenate(pieces[1:], axis=1)]

    splits = max(1, min(SPLITS, owned // 8))
    part = owned // splits
    shape = (masks.shape[0], owned, samples.shape[2], 2 * samples.shape[2])
    branches = [functools.partial(move, mask=m) for m in range(1, top)]

    def forward(mine, arrived):
        return lax.switch(near - 1, branches, jnp.where(crosses, arrived, mine))

    rest = [own[1][k * part : (k + 1) * part] for k in range(splits)]
    far_first_group = move(own[0], far)
    far_rest = [move(r, far) for r in rest]
    near_first_group = forward(own[0], far_first_group)
    total = None
    for k in range(splits):
        start = k * part
        near_rest = forward(rest[k], far_rest[k])
        total = cross_into(
            total, shape, far_place, start, own, [far_first_group, far_rest[k]], [start, 0], factor
        )
        total = cross_into(
            total, shape, near_place, start, own, [near_first_group, near_rest], [start, 0], factor
        )
    return total


def solution(mesh):
    return jax.shard_map(
        on_device,
        mesh=mesh,
        in_specs=(P("hour", None, "chan", None), P()),
        out_specs=P(None, "hour", "chan", None),
        check_vma=False,
    )
```

```python
import functools
import math

import jax
import jax.numpy as jnp
from jax import lax
from jax.experimental import pallas as pl
from jax.experimental.pallas import tpu as pltpu
from jax.sharding import PartitionSpec as P

ROWS = 384
AHEAD = 3


def dft_table(length, bin_count):
    sample_index = lax.broadcasted_iota(jnp.int32, (length, bin_count), 0)
    bin_index = lax.broadcasted_iota(jnp.int32, (length, bin_count), 1)
    phase_angle = (sample_index * bin_index % length).astype(jnp.float32) * (2.0 * math.pi / length)
    return jnp.concatenate([jnp.cos(phase_angle), -jnp.sin(phase_angle)], axis=1).astype(
        jnp.bfloat16
    )


def whiten(series, bin_count):
    dft_rows = dft_table(series.shape[2], bin_count)
    spectrum = jnp.einsum("wcl,lk->kwc", series, dft_rows, preferred_element_type=jnp.float32)
    real_part = spectrum[:bin_count]
    imag_part = spectrum[bin_count:]
    power_mean = jnp.mean(real_part * real_part + imag_part * imag_part, axis=0)
    inverse_rms = lax.rsqrt(power_mean + 1e-06)
    return jnp.concatenate([real_part * inverse_rms, imag_part * inverse_rms], axis=2).astype(
        jnp.bfloat16
    )


def exchange_kernel(mask, far, hours, crosses_ref, own_ref, rest_ref, far_ref, near_ref, stage_ref,
                    hour_send, hour_recv, far_send, far_recv, near_send, near_recv):
    me, hour = lax.axis_index("chan"), lax.axis_index("hour")
    owned = far_ref.shape[1]
    rows = min(ROWS, owned)
    subs = owned // rows
    far_id = (jnp.bitwise_xor(me, far), hour)
    near_id = (jnp.bitwise_xor(me, mask), hour)
    others = [(me, lax.rem(hour + apart, hours)) for apart in range(1, hours)]

    barrier = pltpu.get_barrier_semaphore()
    for target in [far_id, near_id] + others:
        pl.semaphore_signal(barrier, inc=1, device_id=target, device_id_type=pl.DeviceIdType.MESH)
    pl.semaphore_wait(barrier, hours + 1)

    def copy(source, target, send, recv, device):
        return pltpu.make_async_remote_copy(
            src_ref=source, dst_ref=target, send_sem=send, recv_sem=recv,
            device_id=device, device_id_type=pl.DeviceIdType.MESH,
        )

    hour_copies = []
    for apart in range(1, hours):
        for sub in range(subs):
            spot = pl.ds(sub * rows, rows)
            at = (apart - 1) * subs + sub
            hour_copies.append(copy(
                own_ref.at[apart, spot], rest_ref.at[apart - 1, spot],
                hour_send.at[at], hour_recv.at[at], others[apart - 1],
            ))
            hour_copies[-1].start()

    def own_part(c):
        spot = pl.ds(c % subs * rows, rows)
        return own_ref.at[0, spot] if c < subs else rest_ref.at[c // subs - 1, spot]

    total = hours * subs
    far_copies, near_copies = [], []

    def start_far(c):
        if c >= subs:
            hour_copies[c - subs].wait_recv()
        far_copies.append(copy(
            own_part(c), far_ref.at[c // subs, pl.ds(c % subs * rows, rows)],
            far_send.at[c], far_recv.at[c], far_id,
        ))
        far_copies[-1].start()

    for c in range(min(AHEAD, total)):
        start_far(c)
    crosses = crosses_ref[0] != 0
    for c in range(total):
        spot = pl.ds(c % subs * rows, rows)
        far_copies[c].wait_recv()
        stage_ref[c // subs, spot] = jnp.where(
            crosses, far_ref[c // subs, spot], own_part(c)[...]
        )
        near_copies.append(copy(
            stage_ref.at[c // subs, spot], near_ref.at[c // subs, spot],
            near_send.at[c], near_recv.at[c], near_id,
        ))
        near_copies[-1].start()
        if c + AHEAD < total:
            start_far(c + AHEAD)
    for c in range(total):
        near_copies[c].wait_recv()
        near_copies[c].wait_send()
        far_copies[c].wait_send()
    for each in hour_copies:
        each.wait_send()


def exchange(crosses, own, mask, far):
    hours, rows, width = own.shape
    parts = rows // min(ROWS, rows)
    whole = jax.ShapeDtypeStruct(own.shape, own.dtype)
    rest = jax.ShapeDtypeStruct((hours - 1, rows, width), own.dtype)
    vmem = pl.BlockSpec(memory_space=pltpu.VMEM)
    moved = hours * parts
    return pl.pallas_call(
        functools.partial(exchange_kernel, mask, far, hours),
        out_shape=(rest, whole, whole),
        in_specs=[pl.BlockSpec(memory_space=pltpu.SMEM), vmem],
        out_specs=(vmem, vmem, vmem),
        scratch_shapes=[pltpu.VMEM(own.shape, own.dtype)]
        + [pltpu.SemaphoreType.DMA(((hours - 1) * parts,))] * 2
        + [pltpu.SemaphoreType.DMA((moved,))] * 4,
        compiler_params=pltpu.CompilerParams(
            collective_id=mask, has_side_effects=True, vmem_limit_bytes=32 * 1024 * 1024
        ),
        name="exchange",
    )(crosses, own)


def cross_kernel(tile, factor, place_ref, own_ref, rest_ref, far_ref, near_ref, out_ref):
    half = out_ref.shape[2]
    far_place = place_ref[0]

    def one_bin(f, carry):
        def load(ref):
            return [ref[h, f].astype(jnp.float32) for h in range(ref.shape[0])]

        own = load(own_ref) + load(rest_ref)
        left = jnp.concatenate([o[:, :half] for o in own] + [o[:, half:] for o in own], axis=0)
        left = left.astype(jnp.bfloat16)
        for ref, place in ((far_ref, far_place), (near_ref, 1 - far_place)):
            partner = load(ref)
            real_part = [q[:, :half] for q in partner]
            imag_part = [q[:, half:] for q in partner]
            right = jnp.concatenate(
                [
                    jnp.concatenate(real_part + imag_part, axis=0),
                    jnp.concatenate([-q for q in imag_part] + real_part, axis=0),
                ],
                axis=1,
            )
            product = lax.dot_general(
                left,
                right.astype(jnp.bfloat16),
                (((0,), (0,)), ((), ())),
                preferred_element_type=jnp.float32,
            )
            out_ref[place, f] = product * factor
        return carry

    lax.fori_loop(0, tile, one_bin, 0, unroll=True)


def cross(place, own, rest, far, near, factor):
    hours, bins, windows, width = own.shape
    tile = min(8, bins)
    half = width // 2

    def spec(count):
        return pl.BlockSpec((count, tile, windows, width), lambda i, p: (0, i, 0, 0))

    return pl.pallas_call(
        functools.partial(cross_kernel, tile, factor),
        out_shape=jax.ShapeDtypeStruct((2, bins, half, width), jnp.float32),
        grid_spec=pltpu.PrefetchScalarGridSpec(
            num_scalar_prefetch=1,
            grid=(bins // tile,),
            in_specs=[spec(1), spec(hours - 1), spec(hours), spec(hours)],
            out_specs=pl.BlockSpec((2, tile, half, width), lambda i, p: (0, i, 0, 0)),
        ),
        compiler_params=pltpu.CompilerParams(vmem_limit_bytes=32 * 1024 * 1024),
        name="cross",
    )(place, own, rest, far, near)


def on_device(samples, masks):
    windows, channels, length = samples.shape[1:]
    bin_count = length // 2
    hours = lax.axis_size("hour")
    blocks = lax.axis_size("chan")
    owned = bin_count // hours
    factor = 1.0 / math.sqrt(windows * hours)
    far, top = blocks - 1, blocks // 2
    far_first = masks[0] == far
    other = jnp.where(far_first, masks[1], masks[0])
    crosses = other >= top
    near = jnp.where(crosses, other ^ far, other)
    far_place = jnp.where(far_first, 0, 1).astype(jnp.int32).reshape(1)

    spectra = whiten(samples[0], bin_count).reshape(hours, owned * windows, 2 * channels)
    own = jnp.roll(spectra, -lax.axis_index("hour"), axis=0)
    branches = [functools.partial(exchange, mask=m, far=far) for m in range(1, top)]
    moved = lax.switch(near - 1, branches, crosses.astype(jnp.int32).reshape(1), own)
    rest, far_arrived, near_arrived = (
        m.reshape(m.shape[0], owned, windows, 2 * channels) for m in moved
    )
    own = own.reshape(hours, owned, windows, 2 * channels)
    return cross(far_place, own, rest, far_arrived, near_arrived, factor)


def solution(mesh):
    return jax.shard_map(
        on_device,
        mesh=mesh,
        in_specs=(P("hour", None, "chan", None), P()),
        out_specs=P(None, "hour", "chan", None),
        check_vma=False,
    )
```

```python
import functools
import math

import jax
import jax.numpy as jnp
from jax import lax
from jax.experimental import pallas as pl
from jax.experimental.pallas import tpu as pltpu
from jax.sharding import PartitionSpec as P

ROWS = 192
AHEAD = 3


def dft_table(length, bin_count):
    sample_index = lax.broadcasted_iota(jnp.int32, (length, bin_count), 0)
    bin_index = lax.broadcasted_iota(jnp.int32, (length, bin_count), 1)
    phase_angle = (sample_index * bin_index % length).astype(jnp.float32) * (2.0 * math.pi / length)
    return jnp.concatenate([jnp.cos(phase_angle), -jnp.sin(phase_angle)], axis=1).astype(
        jnp.bfloat16
    )


def whiten(series, bin_count):
    dft_rows = dft_table(series.shape[2], bin_count)
    spectrum = jnp.einsum("wcl,lk->kwc", series, dft_rows, preferred_element_type=jnp.float32)
    real_part = spectrum[:bin_count]
    imag_part = spectrum[bin_count:]
    power_mean = jnp.mean(real_part * real_part + imag_part * imag_part, axis=0)
    inverse_rms = lax.rsqrt(power_mean + 1e-06)
    return jnp.concatenate([real_part * inverse_rms, imag_part * inverse_rms], axis=2).astype(
        jnp.bfloat16
    )


def exchange_kernel(mask, far, hours, crosses_ref, own_ref, rest_ref, far_ref, near_ref, stage_ref,
                    hour_send, hour_recv, far_send, far_recv, near_send, near_recv):
    me, hour = lax.axis_index("chan"), lax.axis_index("hour")
    owned = far_ref.shape[1]
    rows = min(ROWS, owned)
    subs = owned // rows
    far_id = (jnp.bitwise_xor(me, far), hour)
    near_id = (jnp.bitwise_xor(me, mask), hour)
    others = [(me, lax.rem(hour + apart, hours)) for apart in range(1, hours)]

    barrier = pltpu.get_barrier_semaphore()
    for target in [far_id, near_id] + others:
        pl.semaphore_signal(barrier, inc=1, device_id=target, device_id_type=pl.DeviceIdType.MESH)
    pl.semaphore_wait(barrier, hours + 1)

    def copy(source, target, send, recv, device):
        return pltpu.make_async_remote_copy(
            src_ref=source, dst_ref=target, send_sem=send, recv_sem=recv,
            device_id=device, device_id_type=pl.DeviceIdType.MESH,
        )

    hour_copies = []
    for apart in range(1, hours):
        for sub in range(subs):
            spot = pl.ds(sub * rows, rows)
            at = (apart - 1) * subs + sub
            hour_copies.append(copy(
                own_ref.at[apart, spot], rest_ref.at[apart - 1, spot],
                hour_send.at[at], hour_recv.at[at], others[apart - 1],
            ))
            hour_copies[-1].start()

    def own_part(c):
        spot = pl.ds(c % subs * rows, rows)
        return own_ref.at[0, spot] if c < subs else rest_ref.at[c // subs - 1, spot]

    total = hours * subs
    far_copies, near_copies = [], []

    def start_far(c):
        if c >= subs:
            hour_copies[c - subs].wait_recv()
        far_copies.append(copy(
            own_part(c), far_ref.at[c // subs, pl.ds(c % subs * rows, rows)],
            far_send.at[c], far_recv.at[c], far_id,
        ))
        far_copies[-1].start()

    for c in range(min(AHEAD, total)):
        start_far(c)
    crosses = crosses_ref[0] != 0
    for c in range(total):
        spot = pl.ds(c % subs * rows, rows)
        far_copies[c].wait_recv()
        stage_ref[c // subs, spot] = jnp.where(
            crosses, far_ref[c // subs, spot], own_part(c)[...]
        )
        near_copies.append(copy(
            stage_ref.at[c // subs, spot], near_ref.at[c // subs, spot],
            near_send.at[c], near_recv.at[c], near_id,
        ))
        near_copies[-1].start()
        if c + AHEAD < total:
            start_far(c + AHEAD)
    for c in range(total):
        near_copies[c].wait_recv()
        near_copies[c].wait_send()
        far_copies[c].wait_send()
    for each in hour_copies:
        each.wait_send()


def exchange(crosses, own, mask, far):
    hours, rows, width = own.shape
    parts = rows // min(ROWS, rows)
    whole = jax.ShapeDtypeStruct(own.shape, own.dtype)
    rest = jax.ShapeDtypeStruct((hours - 1, rows, width), own.dtype)
    vmem = pl.BlockSpec(memory_space=pltpu.VMEM)
    moved = hours * parts
    return pl.pallas_call(
        functools.partial(exchange_kernel, mask, far, hours),
        out_shape=(rest, whole, whole),
        in_specs=[pl.BlockSpec(memory_space=pltpu.SMEM), vmem],
        out_specs=(vmem, vmem, vmem),
        scratch_shapes=[pltpu.VMEM(own.shape, own.dtype)]
        + [pltpu.SemaphoreType.DMA(((hours - 1) * parts,))] * 2
        + [pltpu.SemaphoreType.DMA((moved,))] * 4,
        compiler_params=pltpu.CompilerParams(
            collective_id=mask, has_side_effects=True, vmem_limit_bytes=32 * 1024 * 1024
        ),
        name="exchange",
    )(crosses, own)


def cross_kernel(tile, factor, place_ref, own_ref, rest_ref, far_ref, near_ref, out_ref):
    half = out_ref.shape[2]
    far_place = place_ref[0]

    def one_bin(f, carry):
        def load(ref):
            return [ref[h, f].astype(jnp.float32) for h in range(ref.shape[0])]

        own = load(own_ref) + load(rest_ref)
        left = jnp.concatenate([o[:, :half] for o in own] + [o[:, half:] for o in own], axis=0)
        left = left.astype(jnp.bfloat16)
        for ref, place in ((far_ref, far_place), (near_ref, 1 - far_place)):
            partner = load(ref)
            real_part = [q[:, :half] for q in partner]
            imag_part = [q[:, half:] for q in partner]
            right = jnp.concatenate(
                [
                    jnp.concatenate(real_part + imag_part, axis=0),
                    jnp.concatenate([-q for q in imag_part] + real_part, axis=0),
                ],
                axis=1,
            )
            product = lax.dot_general(
                left,
                right.astype(jnp.bfloat16),
                (((0,), (0,)), ((), ())),
                preferred_element_type=jnp.float32,
            )
            out_ref[place, f] = product * factor
        return carry

    lax.fori_loop(0, tile, one_bin, 0, unroll=True)


def cross(place, own, rest, far, near, factor):
    hours, bins, windows, width = own.shape
    tile = min(8, bins)
    half = width // 2

    def spec(count):
        return pl.BlockSpec((count, tile, windows, width), lambda i, p: (0, i, 0, 0))

    return pl.pallas_call(
        functools.partial(cross_kernel, tile, factor),
        out_shape=jax.ShapeDtypeStruct((2, bins, half, width), jnp.float32),
        grid_spec=pltpu.PrefetchScalarGridSpec(
            num_scalar_prefetch=1,
            grid=(bins // tile,),
            in_specs=[spec(1), spec(hours - 1), spec(hours), spec(hours)],
            out_specs=pl.BlockSpec((2, tile, half, width), lambda i, p: (0, i, 0, 0)),
        ),
        compiler_params=pltpu.CompilerParams(vmem_limit_bytes=32 * 1024 * 1024),
        name="cross",
    )(place, own, rest, far, near)


def on_device(samples, masks):
    windows, channels, length = samples.shape[1:]
    bin_count = length // 2
    hours = lax.axis_size("hour")
    blocks = lax.axis_size("chan")
    owned = bin_count // hours
    factor = 1.0 / math.sqrt(windows * hours)
    far, top = blocks - 1, blocks // 2
    far_first = masks[0] == far
    other = jnp.where(far_first, masks[1], masks[0])
    crosses = other >= top
    near = jnp.where(crosses, other ^ far, other)
    far_place = jnp.where(far_first, 0, 1).astype(jnp.int32).reshape(1)

    spectra = whiten(samples[0], bin_count).reshape(hours, owned * windows, 2 * channels)
    own = jnp.roll(spectra, -lax.axis_index("hour"), axis=0)
    branches = [functools.partial(exchange, mask=m, far=far) for m in range(1, top)]
    moved = lax.switch(near - 1, branches, crosses.astype(jnp.int32).reshape(1), own)
    rest, far_arrived, near_arrived = (
        m.reshape(m.shape[0], owned, windows, 2 * channels) for m in moved
    )
    own = own.reshape(hours, owned, windows, 2 * channels)
    return cross(far_place, own, rest, far_arrived, near_arrived, factor)


def solution(mesh):
    return jax.shard_map(
        on_device,
        mesh=mesh,
        in_specs=(P("hour", None, "chan", None), P()),
        out_specs=P(None, "hour", "chan", None),
        check_vma=False,
    )
```
